512 devices in a mesh: vox: 64 (over z, x_hi, core), tm: 4 (over y), mod: 2 (over x_lo).
Axes of the slice: x: 4 (x_hi: 2, x_lo: 2; x = x_hi * 2 + x_lo), y: 4, z: 16, core: 2. Of those that a mesh axis runs over, the one named last changes fastest.
Arguments:
- scans: bfloat16 [2, 16384, 48, 512], P('mod', 'vox', None, 'tm'), may hold values from -6 to 6
- spatial_init: float32 [2, 16384, 128], P('mod', 'vox'), may hold values from -6 to 6
- time_init: float32 [512, 128], P('tm'), may hold values from -0.09375 to 0.09375
- subject_init: float32 [48, 128], replicated, may hold values from -6 to 6
- hrf_kernel: float32 [16], replicated, may hold values from 0.05 to 0.5
- kept_blocks: int32 [48, 32], P(None, 'tm'), may hold values 0 or 1
Outputs:
- spatial_factors: float32 [2, 16384, 128], P('mod', 'vox')
- time_factors: float32 [512, 128], P('tm')
- subject_factors: float32 [48, 128], replicated
The draws below stay inside these ranges and needn't reach their ends.
All inputs are finite; a program needn't handle non-finite values. No bound on the sum of `kept_blocks` on one device may be relied on, other than what follows from the above.
Results may differ from the reference program's by a relative error of at most 0.003.
Values sent between devices are 32-bit elements; how exact they have to be, the bound alone decides.
A program may use at most 64 MiB of HBM per device.

```python
import math
import jax
import jax.numpy as jnp
from jax import lax

RANK = 128
ROW_DEV = 256
SUBJ = 48
KH = 16
BLOCK = 16
ROWS = 16384
TRS = 512


def touch_ends(entries, key, smallest, high):
    shape = entries.shape
    index_at = [jax.random.randint(jax.random.fold_in(key, axis), (), 0, shape[axis]) for axis in range(len(shape))]
    entries = entries.at[tuple(index_at)].set(smallest)
    longest = shape.index(max(shape))
    index_at[longest] = (index_at[longest] + 1) % shape[longest]
    return entries.at[tuple(index_at)].set(high)


def shard_levels(rng, extent, pieces, smallest, high):
    def one(dim, shards_of):
        heights = jax.random.uniform(jax.random.fold_in(jax.random.fold_in(rng, 6), dim), (shards_of,), jnp.float32, smallest / len(pieces), high / len(pieces))
        return jnp.repeat(jnp.exp(heights), extent[dim] // shards_of).reshape((-1,) + (1,) * (len(extent) - dim - 1))

    level = one(*pieces[0])
    for cut in pieces[1:]:
        level = level * one(*cut)
    return level


def gaussian(stream_key, dims, scale, limit, cuts=(), kind=jnp.bfloat16):
    drawn = jax.random.normal(stream_key, dims, jnp.float32) * scale
    if len(cuts) > 0:
        drawn = shard_levels(stream_key, dims, cuts, -0.22, 0.18) * drawn
    return jnp.clip(drawn, min=-limit, max=limit).astype(kind)


def setup_inputs(seed: int = 0) -> dict:
    key_list = jax.random.split(jax.random.key(seed), 7)
    scans = gaussian(key_list[0], (2, ROWS, SUBJ, TRS), 1.0, 6.0, ((0, 2), (1, 64), (3, 4)))
    spatial_init = gaussian(key_list[1], (2, ROWS, RANK), 1.0, 6.0, ((0, 2), (1, 64)), jnp.float32)
    time_init = gaussian(key_list[2], (TRS, RANK), ((SUBJ * TRS) ** -0.5), 0.09375, ((0, 4),), jnp.float32)
    subject_init = gaussian(key_list[3], (SUBJ, RANK), 1.0, 6.0, (), jnp.float32)
    hrf_kernel = jnp.clip(jnp.exp(jax.random.uniform(key_list[4], (KH,), jnp.float32, math.log(0.05), math.log(0.5))), 0.05, 0.5)
    kept_blocks = touch_ends((jax.random.randint(key_list[5], (SUBJ, TRS // BLOCK), 0, 4) < 3).astype(jnp.int32), jax.random.fold_in(key_list[5], 1), 0, 1)
    return {"scans": scans, "spatial_init": spatial_init, "time_init": time_init, "subject_init": subject_init, "hrf_kernel": hrf_kernel, "kept_blocks": kept_blocks}


RIDGE = 0.1
EPS = 1e-06

def conv_causal(series, kernel):
    reach = kernel.shape[0]
    count = series.shape[0]
    padded = jnp.concatenate([jnp.zeros((reach - 1, series.shape[1]), series.dtype), series])
    summed = jnp.zeros_like(series)
    for lag in range(reach):
        summed = summed + kernel[lag] * padded[reach - 1 - lag:reach - 1 - lag + count]
    return summed

def conv_adjoint(series, kernel):
    reach = kernel.shape[0]
    count = series.shape[0]
    padded = jnp.concatenate([series, jnp.zeros((reach - 1, series.shape[1]), series.dtype)])
    summed = jnp.zeros_like(series)
    for lag in range(reach):
        summed = summed + kernel[lag] * padded[lag:lag + count]
    return summed

def ridge_solve(right_side, gram):
    eye_mat = jnp.eye(gram.shape[0], dtype=gram.dtype)
    factor = jnp.linalg.cholesky(gram + RIDGE * eye_mat)
    return jax.scipy.linalg.cho_solve((factor, True), right_side.T).T

def hgram(left, right):
    return jnp.dot(left.T, right, precision=lax.Precision.HIGHEST)

def fill_rows(signal, previous, khatri, kept_flat, modality):
    if modality == 0:
        modeled = lax.dot_general(previous.astype(jnp.bfloat16).astype(jnp.float32), khatri.astype(jnp.float32), (((1,), (1,)), ((), ())), preferred_element_type=jnp.float32)
        return jnp.where(kept_flat[None, :], signal.astype(jnp.float32), modeled).astype(jnp.bfloat16)
    return signal

def reference(scans, spatial_init, time_init, subject_init, hrf_kernel, kept_blocks):
    nblocks = ROWS // ROW_DEV
    kept_tr = jnp.repeat(kept_blocks, BLOCK, axis=1) > 0
    kept_flat = kept_tr.reshape(SUBJ * TRS)
    factors = [conv_causal(time_init, hrf_kernel), time_init]
    subj_gram = hgram(subject_init, subject_init)
    new_spatial = []
    projections = []
    row_grams = []
    khatris = []
    for modality in range(2):
        factor_t = factors[modality]
        khatri = (subject_init[:, None, :] * factor_t[None, :, :]).astype(jnp.bfloat16).reshape(SUBJ * TRS, RANK)
        khatris.append(khatri)
        gram_a = subj_gram * hgram(factor_t, factor_t)
        signal_blocks = scans[modality].reshape(nblocks, ROW_DEV, SUBJ * TRS)
        prev_blocks = spatial_init[modality].reshape(nblocks, ROW_DEV, RANK)

        def first_pass(items, khatri=khatri, gram_a=gram_a, modality=modality):
            signal, previous = items
            filled = fill_rows(signal, previous, khatri, kept_flat, modality)
            mttkrp = jnp.dot(filled.astype(jnp.float32), khatri.astype(jnp.float32), preferred_element_type=jnp.float32)
            updated = ridge_solve(mttkrp, gram_a)
            khatri2 = (updated[:, None, :] * subject_init[None, :, :]).astype(jnp.bfloat16).reshape(ROW_DEV * SUBJ, RANK)
            proj = lax.dot_general(filled.reshape(ROW_DEV * SUBJ, TRS).astype(jnp.float32), khatri2.astype(jnp.float32), (((0,), (0,)), ((), ())), preferred_element_type=jnp.float32)
            return (updated, proj, hgram(updated, updated))
        updated, proj, grams = lax.map(first_pass, (signal_blocks, prev_blocks))
        new_spatial.append(updated.reshape(ROWS, RANK))
        projections.append(lax.optimization_barrier(jnp.sum(proj, axis=0)))
        row_grams.append(lax.optimization_barrier(jnp.sum(grams, axis=0)))
    time_rhs = conv_adjoint(projections[0], hrf_kernel) + projections[1]
    raw = ROWS * ridge_solve(time_rhs, (row_grams[0] + row_grams[1]) * subj_gram)
    time_factors = raw / jnp.sqrt(lax.optimization_barrier(jnp.mean(raw * raw, axis=0)) + EPS)
    scale_c = (2.0 * ROWS * TRS) ** (-0.5)
    scaled_eeg = time_factors * scale_c
    scaled = [conv_causal(scaled_eeg, hrf_kernel), scaled_eeg]
    subject_rhs = jnp.zeros((SUBJ, RANK), jnp.float32)
    gram_c = jnp.zeros((RANK, RANK), jnp.float32)
    for modality in range(2):
        signal_blocks = scans[modality].reshape(nblocks, ROW_DEV, SUBJ * TRS)
        prev_blocks = spatial_init[modality].reshape(nblocks, ROW_DEV, RANK)
        new_blocks = new_spatial[modality].reshape(nblocks, ROW_DEV, RANK)
        scaled_t = scaled[modality]

        def second_pass(items, khatri=khatris[modality], scaled_t=scaled_t, modality=modality):
            signal, previous, updated = items
            filled = fill_rows(signal, previous, khatri, kept_flat, modality)
            khatri3 = (updated[:, None, :] * scaled_t[None, :, :]).astype(jnp.bfloat16)
            return lax.dot_general(filled.reshape(ROW_DEV, SUBJ, TRS).astype(jnp.float32), khatri3.astype(jnp.float32), (((0, 2), (0, 1)), ((), ())), preferred_element_type=jnp.float32)
        parts = lax.map(second_pass, (signal_blocks, prev_blocks, new_blocks))
        subject_rhs = subject_rhs + lax.optimization_barrier(jnp.sum(parts, axis=0))
        gram_c = gram_c + row_grams[modality] * hgram(scaled_t, scaled_t)
    subject_factors = ridge_solve(subject_rhs, gram_c)
    spatial_factors = jnp.stack(new_spatial)
    return (spatial_factors, time_factors, subject_factors)
```

```python
import functools

import jax
import jax.numpy as jnp
from jax import lax
from jax.experimental import pallas as pl
from jax.experimental.pallas import tpu as pltpu
from jax.sharding import PartitionSpec as P

RIDGE = 0.1
EPS = 1e-06
MESH = pl.DeviceIdType.MESH
PLANE = 4
HIGHEST = lax.Precision.HIGHEST


def dot(a, b):
    return jnp.dot(a, b, precision=HIGHEST, preferred_element_type=jnp.float32)


def tdot(a, b):
    return lax.dot_general(
        a, b, (((0,), (0,)), ((), ())), precision=HIGHEST, preferred_element_type=jnp.float32
    )


def spd_inverse(gram):
    n = gram.shape[0]
    lane = lax.broadcasted_iota(jnp.int32, (8, n), 1)
    sub = lax.broadcasted_iota(jnp.int32, (8, n), 0)
    eye8 = jnp.where(lane == sub, 1.0, 0.0)
    inside = lane < 8
    ridge = jnp.where(
        lax.broadcasted_iota(jnp.int32, (n, n), 0) == lax.broadcasted_iota(jnp.int32, (n, n), 1),
        RIDGE,
        0.0,
    )

    def step(_, mat):
        top = mat[0:8]
        cols = [jnp.broadcast_to(top[:, j : j + 1], (8, n)) for j in range(8)]
        row = jnp.where(inside, eye8, top)
        for i in range(8):
            gain = jnp.where(sub == i, -1.0, cols[i]) * (1.0 / cols[i][i : i + 1])
            row = jnp.where(sub == i, 0.0, row) - gain * row[i : i + 1]
            for j in range(i + 1, 8):
                cols[j] = jnp.where(sub == i, 0.0, cols[j]) - gain * cols[j][i : i + 1]
        rows = []
        for b in range(1, n // 8):
            below = mat[8 * b : 8 * b + 8]
            left = jnp.where(inside, 0.0, below)
            for j in range(8):
                left = left - jnp.broadcast_to(below[:, j : j + 1], (8, n)) * row[j : j + 1]
            rows.append(left)
        return pltpu.roll(jnp.concatenate(rows + [row]), n - 8, 1)

    return lax.fori_loop(0, n // 8, step, gram + ridge, unroll=2)


def sweep(
    sizes,
    scans,
    spatial,
    time_init,
    subject,
    hrf,
    kept,
    out_spatial,
    out_time,
    out_subject,
    x_in,
    x_f32,
    xs,
    mask,
    pad,
    factors,
    rhs,
    rhs_in,
    updated,
    gram_part,
    g1,
    g2,
    g_sum,
    g_all,
    ppad,
    ext,
    halo,
    r1,
    r2,
    r_sum,
    r_all,
    s_part,
    s1,
    s2,
    s_sum,
    s_own,
    s_all,
    local_sem,
    send_sem,
    recv_sem,
    halo_sem,
):
    nz, ntm, nmod = sizes
    rows, rank = spatial.shape
    subjects = subject.shape[0]
    trs = time_init.shape[0]
    reach = hrf.shape[0]
    vox, tm, mod = lax.axis_index("vox"), lax.axis_index("tm"), lax.axis_index("mod")
    z, c4 = vox // PLANE, vox % PLANE
    nplane = PLANE * ntm * nmod
    place = (c4 * ntm + tm) * nmod + mod
    ngram = PLANE * ntm
    gplace = c4 * ntm + tm
    nrhs = PLANE * nmod
    rplace = c4 * nmod + mod
    grow = rank // ngram
    rrow = trs // nrhs
    srow = subjects // nz
    own = pl.ds(pl.multiple_of(trs * tm, trs), trs)
    part = rows // ntm
    my_part = pl.ds(pl.multiple_of(part * tm, part), part)

    def along_tm(d):
        return (vox, lax.rem(tm + d, ntm), mod)

    def along_z(d):
        return (lax.rem(z + d, nz) * PLANE + c4, tm, mod)

    def in_plane(d):
        to = lax.rem(place + d, nplane)
        return (z * PLANE + to // (ntm * nmod), lax.rem(to // nmod, ntm), lax.rem(to, nmod))

    def send(stage, src, dst, device):
        pltpu.make_async_remote_copy(
            src_ref=src,
            dst_ref=dst,
            send_sem=send_sem.at[stage],
            recv_sem=recv_sem.at[stage],
            device_id=device,
            device_id_type=MESH,
        ).start()

    def every(count, body):
        def step(d, carry):
            body(d)
            return carry

        lax.fori_loop(1, count, step, 0)

    def wait(sem, stage, ref):
        pltpu.make_async_copy(ref, ref, sem.at[stage]).wait()

    load = pltpu.make_async_copy(scans, x_in, local_sem)
    load.start()
    barrier = pltpu.get_barrier_semaphore()
    every(
        nplane,
        lambda d: pl.semaphore_signal(barrier, 1, device_id=in_plane(d), device_id_type=MESH),
    )
    every(
        nz, lambda d: pl.semaphore_signal(barrier, 1, device_id=along_z(d), device_id_type=MESH)
    )
    pl.semaphore_wait(barrier, nplane + nz - 2)

    pad[0:reach] = jnp.zeros((reach, rank), jnp.float32)
    own_pad = pl.ds(pl.multiple_of(reach + trs * tm, 8), trs)
    every(ntm, lambda d: send(0, time_init, pad.at[own_pad], along_tm(d)))

    load.wait()

    def widen(i, carry):
        at = pl.ds(pl.multiple_of(i * 512, 512), 512)
        x_f32[at] = x_in[at].astype(jnp.float32)
        return carry

    lax.fori_loop(0, rows * subjects // 512, widen, 0)

    def regroup(s, carry):
        xs[pl.ds(pl.multiple_of(s * rows, rows), rows)] = x_f32[
            pl.ds(s, rows, subjects), :
        ].astype(jnp.bfloat16)
        return carry

    lax.fori_loop(0, subjects, regroup, 0)
    block = trs // kept.shape[1]
    block_of = lax.broadcasted_iota(jnp.int32, (subjects, trs), 1) // block
    flags = kept[...]
    keep = jnp.zeros((subjects, trs), jnp.int32)
    for b in range(kept.shape[1]):
        keep = jnp.where(block_of == b, flags[:, b : b + 1], keep)
    mask[...] = jnp.where(mod == 0, keep, 1).astype(jnp.float32)
    subj = subject[...]
    subj_gram = tdot(subj, subj)
    previous = spatial[...].astype(jnp.bfloat16)
    is_fmri = mod == 0
    lags = [hrf[k] for k in range(reach)]
    taps = [jnp.where(is_fmri, lags[k], 1.0 if k == 0 else 0.0) for k in range(reach)]

    pad[own_pad] = time_init[...]
    wait(recv_sem, 0, pad.at[pl.ds(reach, (ntm - 1) * trs)])

    def conv(weights, base):
        summed = weights[0] * pad[reach + base : reach + base + trs]
        for k in range(1, reach):
            summed = summed + weights[k] * pad[reach + base - k : reach + base - k + trs]
        return summed

    for i in range(ntm):
        factors[i * trs : (i + 1) * trs] = conv(taps, i * trs)
    factor = factors[own]
    everything = factors[...]
    time_gram = tdot(everything, everything)

    rhs[...] = jnp.zeros_like(rhs)

    def fill(i, carry):
        s = 2 * i
        first = pl.ds(pl.multiple_of(s * rows, rows), rows)
        second = pl.ds(pl.multiple_of((s + 1) * rows, rows), rows)
        khatri = jnp.concatenate(
            [
                (subject[pl.ds(s, 1)] * factor).astype(jnp.bfloat16),
                (subject[pl.ds(s + 1, 1)] * factor).astype(jnp.bfloat16),
            ]
        )
        modeled = lax.dot_general(
            previous, khatri, (((1,), (1,)), ((), ())), preferred_element_type=jnp.float32
        )
        f0 = jnp.where(
            mask[pl.ds(s, 1)] > 0, xs[first].astype(jnp.float32), modeled[:, :trs]
        ).astype(jnp.bfloat16)
        f1 = jnp.where(
            mask[pl.ds(s + 1, 1)] > 0, xs[second].astype(jnp.float32), modeled[:, trs:]
        ).astype(jnp.bfloat16)
        xs[first] = f0
        xs[second] = f1
        rhs[...] += jnp.dot(
            jnp.concatenate([f0, f1], axis=1), khatri, preferred_element_type=jnp.float32
        )
        return carry

    lax.fori_loop(0, subjects // 2, fill, 0)

    def scatter_rows(d):
        to = pl.multiple_of(part * lax.rem(tm + d, ntm), part)
        send(1, rhs.at[pl.ds(to, part)], rhs_in.at[d - 1], along_tm(d))

    every(ntm, scatter_rows)
    inverse = spd_inverse(subj_gram * time_gram)
    wait(recv_sem, 1, rhs_in)
    mine = rhs[my_part]
    for d in range(ntm - 1):
        mine = mine + rhs_in[d]
    solved = dot(mine, inverse)
    updated[my_part] = solved
    every(ntm, lambda d: send(2, updated.at[my_part], updated.at[my_part], along_tm(d)))

    gram_part[...] = tdot(solved, solved)

    def scatter_gram(d):
        to = lax.rem(gplace + d, ngram)
        send(
            3,
            gram_part.at[pl.ds(pl.multiple_of(grow * to, grow), grow)],
            g1.at[d - 1],
            (z * PLANE + to // ntm, lax.rem(to, ntm), mod),
        )

    every(ngram, scatter_gram)
    wait(recv_sem, 2, updated.at[pl.ds(0, (ntm - 1) * part)])
    upd = updated[...]
    out_spatial[...] = upd

    wait(recv_sem, 3, g1)
    mine = gram_part[pl.ds(pl.multiple_of(grow * gplace, grow), grow)]
    for d in range(ngram - 1):
        mine = mine + g1[d]
    g2[z] = mine
    every(nz, lambda d: send(4, g2.at[z], g2.at[z], along_z(d)))

    def project(i, proj):
        s = 2 * i
        khatri = jnp.concatenate(
            [
                (upd * subject[pl.ds(s, 1)]).astype(jnp.bfloat16),
                (upd * subject[pl.ds(s + 1, 1)]).astype(jnp.bfloat16),
            ]
        )
        filled = xs[pl.ds(pl.multiple_of(s * rows, rows), 2 * rows)]
        return proj + lax.dot_general(
            filled, khatri, (((0,), (0,)), ((), ())), preferred_element_type=jnp.float32
        )

    proj = lax.fori_loop(0, subjects // 2, project, jnp.zeros((trs, rank), jnp.float32))
    ppad[0:reach] = jnp.zeros((reach, rank), jnp.float32)
    ppad[reach : reach + trs] = proj
    ppad[reach + trs :] = jnp.zeros((reach, rank), jnp.float32)
    spread = taps[0] * ppad[0 : reach + trs]
    for k in range(1, reach):
        spread = spread + taps[k] * ppad[k : k + reach + trs]
    ext[...] = spread

    def scatter_time(d):
        to = lax.rem(rplace + d, nrhs)
        send(
            6,
            ext.at[pl.ds(pl.multiple_of(reach + rrow * to, 8), rrow)],
            r1.at[d - 1],
            (z * PLANE + to // nmod, tm, lax.rem(to, nmod)),
        )

    every(nrhs, scatter_time)
    gives_halo = jnp.logical_and(is_fmri, tm > 0)
    takes_halo = jnp.logical_and(rplace == nrhs - 1, tm < ntm - 1)
    halo_copy = pltpu.make_async_remote_copy(
        src_ref=ext.at[pl.ds(0, rrow)],
        dst_ref=halo.at[c4],
        send_sem=halo_sem.at[0],
        recv_sem=halo_sem.at[1],
        device_id=(z * PLANE + PLANE - 1, lax.rem(tm + ntm - 1, ntm), nmod - 1),
        device_id_type=MESH,
    )
    halo_all = pltpu.make_async_copy(halo, halo, halo_sem.at[1])

    @pl.when(gives_halo)
    def _():
        halo_copy.start()

    wait(recv_sem, 4, g2.at[pl.ds(0, nz - 1)])
    mine = g2[0]
    for i in range(1, nz):
        mine = mine + g2[i]
    g_sum[...] = mine
    g_own = mod * ngram + gplace
    g_all[g_own] = mine
    every(nplane, lambda d: send(5, g_sum, g_all.at[g_own], in_plane(d)))

    wait(recv_sem, 6, r1)
    mine = ext[pl.ds(pl.multiple_of(reach + rrow * rplace, 8), rrow)]
    for d in range(nrhs - 1):
        mine = mine + r1[d]
    r2[z] = mine

    @pl.when(takes_halo)
    def _():
        halo_all.wait()
        total = r2[z]
        for i in range(PLANE):
            total = total + halo[i]
        r2[z] = total

    every(nz, lambda d: send(7, r2.at[z], r2.at[z], along_z(d)))

    wait(recv_sem, 5, g_all.at[pl.ds(0, nplane - 1)])
    grams = [
        jnp.concatenate([g_all[m * ngram + i] for i in range(ngram)]) for m in range(nmod)
    ]
    inverse = spd_inverse((grams[0] + grams[1]) * subj_gram)

    wait(recv_sem, 7, r2.at[pl.ds(0, nz - 1)])
    mine = r2[0]
    for i in range(1, nz):
        mine = mine + r2[i]
    r_sum[...] = mine
    r_own = tm * nrhs + rplace
    r_all[r_own] = mine
    every(nplane, lambda d: send(8, r_sum, r_all.at[r_own], in_plane(d)))
    wait(recv_sem, 8, r_all.at[pl.ds(0, nplane - 1)])
    right = jnp.concatenate([r_all[i] for i in range(ntm * nrhs)])
    raw = (rows * nz * PLANE) * dot(right, inverse)
    mean = jnp.sum(raw * raw, axis=0, keepdims=True) / (ntm * trs)
    fresh = raw / jnp.sqrt(mean + EPS)
    scale_c = (2.0 * rows * nz * PLANE * trs * ntm) ** (-0.5)
    pad[reach:] = fresh
    out_time[...] = pad[own_pad]
    pad[reach:] = fresh * scale_c
    for i in range(ntm):
        factors[i * trs : (i + 1) * trs] = conv(lags, i * trs)
    scaled = jnp.where(is_fmri, factors[own], pad[own_pad])
    high = scaled.astype(jnp.bfloat16)
    low = (scaled - high.astype(jnp.float32)).astype(jnp.bfloat16)
    halves = jnp.concatenate([high, low], axis=1)

    def contract(i, carry):
        lines = []
        for j in range(srow):
            s = i * srow + j
            both = jnp.dot(
                xs[pl.ds(pl.multiple_of(s * rows, rows), rows)],
                halves,
                preferred_element_type=jnp.float32,
            )
            lines.append(
                jnp.sum((both[:, :rank] + both[:, rank:]) * upd, axis=0, keepdims=True)
            )
        s_part[i] = jnp.concatenate(lines)
        return carry

    lax.fori_loop(0, nz, contract, 0)
    every(nz, lambda d: send(9, s_part.at[lax.rem(z + d, nz)], s1.at[d - 1], along_z(d)))
    eeg = pad[reach:]
    fmri = factors[...]
    gram_c = grams[0] * tdot(fmri, fmri) + grams[1] * tdot(eeg, eeg)

    wait(recv_sem, 9, s1)
    mine = s_part[z]
    for d in range(nz - 1):
        mine = mine + s1[d]
    s_own[...] = mine
    s2[place] = mine
    every(nplane, lambda d: send(10, s_own, s2.at[place], in_plane(d)))
    inverse = spd_inverse(gram_c)
    wait(recv_sem, 10, s2.at[pl.ds(0, nplane - 1)])
    mine = s2[0]
    for i in range(1, nplane):
        mine = mine + s2[i]
    s_sum[...] = mine
    s_all[z] = mine
    every(nz, lambda d: send(11, s_sum, s_all.at[z], along_z(d)))
    wait(recv_sem, 11, s_all.at[pl.ds(0, nz - 1)])
    out_subject[...] = dot(jnp.concatenate([s_all[i] for i in range(nz)]), inverse)

    wait(send_sem, 0, pad.at[pl.ds(reach, (ntm - 1) * trs)])
    wait(send_sem, 1, rhs_in)
    wait(send_sem, 2, updated.at[pl.ds(0, (ntm - 1) * part)])
    wait(send_sem, 3, g1)
    wait(send_sem, 4, g2.at[pl.ds(0, nz - 1)])
    wait(send_sem, 5, g_all.at[pl.ds(0, nplane - 1)])
    wait(send_sem, 6, r1)
    wait(send_sem, 7, r2.at[pl.ds(0, nz - 1)])
    wait(send_sem, 8, r_all.at[pl.ds(0, nplane - 1)])
    wait(send_sem, 9, s1)
    wait(send_sem, 10, s2.at[pl.ds(0, nplane - 1)])
    wait(send_sem, 11, s_all.at[pl.ds(0, nz - 1)])

    @pl.when(gives_halo)
    def _():
        halo_copy.wait_send()


def per_device(scans, spatial_init, time_init, subject_init, hrf_kernel, kept_blocks):
    nz = lax.axis_size("vox") // PLANE
    ntm, nmod = lax.axis_size("tm"), lax.axis_size("mod")
    _, rows, subjects, trs = scans.shape
    rank = subject_init.shape[1]
    reach = hrf_kernel.shape[0]
    nplane, ngram, nrhs = PLANE * ntm * nmod, PLANE * ntm, PLANE * nmod
    grow, rrow, srow = rank // ngram, trs // nrhs, subjects // nz
    f32, bf16 = jnp.float32, jnp.bfloat16
    vmem = pl.BlockSpec(memory_space=pltpu.VMEM)
    updated, time_factors, subject_factors = pl.pallas_call(
        functools.partial(sweep, (nz, ntm, nmod)),
        out_shape=(
            jax.ShapeDtypeStruct((rows, rank), f32),
            jax.ShapeDtypeStruct((trs, rank), f32),
            jax.ShapeDtypeStruct((subjects, rank), f32),
        ),
        in_specs=[
            pl.BlockSpec(memory_space=pl.ANY),
            vmem,
            vmem,
            vmem,
            pl.BlockSpec(memory_space=pltpu.SMEM),
            vmem,
        ],
        out_specs=(vmem, vmem, vmem),
        scratch_shapes=[
            pltpu.VMEM((rows * subjects, trs), bf16),
            pltpu.VMEM((rows * subjects, trs), f32),
            pltpu.VMEM((subjects * rows, trs), bf16),
            pltpu.VMEM((subjects, trs), f32),
            pltpu.VMEM((reach + ntm * trs, rank), f32),
            pltpu.VMEM((ntm * trs, rank), f32),
            pltpu.VMEM((rows, rank), f32),
            pltpu.VMEM((ntm - 1, rows // ntm, rank), f32),
            pltpu.VMEM((rows, rank), f32),
            pltpu.VMEM((rank, rank), f32),
            pltpu.VMEM((ngram - 1, grow, rank), f32),
            pltpu.VMEM((nz, grow, rank), f32),
            pltpu.VMEM((grow, rank), f32),
            pltpu.VMEM((nplane, grow, rank), f32),
            pltpu.VMEM((2 * reach + trs, rank), f32),
            pltpu.VMEM((reach + trs, rank), f32),
            pltpu.VMEM((PLANE, rrow, rank), f32),
            pltpu.VMEM((nrhs - 1, rrow, rank), f32),
            pltpu.VMEM((nz, rrow, rank), f32),
            pltpu.VMEM((rrow, rank), f32),
            pltpu.VMEM((nplane, rrow, rank), f32),
            pltpu.VMEM((nz, srow, rank), f32),
            pltpu.VMEM((nz - 1, srow, rank), f32),
            pltpu.VMEM((nplane, srow, rank), f32),
            pltpu.VMEM((srow, rank), f32),
            pltpu.VMEM((srow, rank), f32),
            pltpu.VMEM((nz, srow, rank), f32),
            pltpu.SemaphoreType.DMA,
            pltpu.SemaphoreType.DMA((12,)),
            pltpu.SemaphoreType.DMA((12,)),
            pltpu.SemaphoreType.DMA((2,)),
        ],
        compiler_params=pltpu.CompilerParams(
            collective_id=0, has_side_effects=True, vmem_limit_bytes=48 * 1024 * 1024
        ),
        name="sweep",
    )(
        scans.reshape(rows * subjects, trs),
        spatial_init[0],
        time_init,
        subject_init,
        hrf_kernel,
        kept_blocks,
    )
    return updated[None], time_factors, subject_factors


def solution(mesh):
    return jax.shard_map(
        per_device,
        mesh=mesh,
        in_specs=(
            P("mod", "vox", None, "tm"),
            P("mod", "vox", None),
            P("tm", None),
            P(),
            P(),
            P(None, "tm"),
        ),
        out_specs=(P("mod", "vox", None), P("tm", None), P()),
        check_vma=False,
    )
```

```python
import functools
import math

import jax
import jax.numpy as jnp
from jax import lax
from jax.experimental import pallas as pl
from jax.experimental.pallas import tpu as pltpu
from jax.sharding import PartitionSpec as P

RIDGE = 0.1
EPS = 1e-06
MESH = pl.DeviceIdType.MESH
PLANE = 4
HIGHEST = lax.Precision.HIGHEST


def dot(a, b):
    return jnp.dot(a, b, precision=HIGHEST, preferred_element_type=jnp.float32)


def tdot(a, b):
    return lax.dot_general(
        a, b, (((0,), (0,)), ((), ())), precision=HIGHEST, preferred_element_type=jnp.float32
    )


def ridged(gram):
    n = gram.shape[0]
    at = [lax.broadcasted_iota(jnp.int32, (n, n), d) for d in range(2)]
    return gram + jnp.where(at[0] == at[1], RIDGE, 0.0)


def eliminate(mat):
    n = mat.shape[0]
    lane = lax.broadcasted_iota(jnp.int32, (8, n), 1)
    sub = lax.broadcasted_iota(jnp.int32, (8, n), 0)
    inside = lane < 8
    top = mat[0:8]
    cols = [jnp.broadcast_to(top[:, j : j + 1], (8, n)) for j in range(8)]
    row = jnp.where(inside, jnp.where(lane == sub, 1.0, 0.0), top)
    for i in range(8):
        gain = jnp.where(sub == i, -1.0, cols[i]) * (1.0 / cols[i][i : i + 1])
        row = jnp.where(sub == i, 0.0, row) - gain * row[i : i + 1]
        for j in range(i + 1, 8):
            cols[j] = jnp.where(sub == i, 0.0, cols[j]) - gain * cols[j][i : i + 1]
    rows = []
    for b in range(1, n // 8):
        below = mat[8 * b : 8 * b + 8]
        left = jnp.where(inside, 0.0, below)
        for j in range(8):
            left = left - jnp.broadcast_to(below[:, j : j + 1], (8, n)) * row[j : j + 1]
        rows.append(left)
    return pltpu.roll(jnp.concatenate(rows + [row]), n - 8, 1)


def eliminations(count, mat):
    return lax.fori_loop(0, count, lambda _, m: eliminate(m), mat, unroll=2)


def sweep(
    sizes,
    scans,
    spatial_in,
    time_init,
    subject_in,
    hrf,
    kept_in,
    out_spatial,
    out_time,
    out_subject,
    spatial,
    subject,
    kept,
    win,
    x_in,
    x_f32,
    xs,
    mask,
    pad,
    factors,
    rhs,
    rhs_in,
    updated,
    gram_part,
    g1,
    g2,
    g_sum,
    g_all,
    ppad,
    ext,
    halo,
    r1,
    r2,
    r_sum,
    r_all,
    s_part,
    s1,
    s2,
    s_sum,
    s_all,
    local_sem,
    send_sem,
    recv_sem,
    halo_sem,
):
    nz, ntm, nmod = sizes
    rows, rank = spatial.shape
    subjects = subject.shape[0]
    trs = time_init.shape[0]
    reach = hrf.shape[0]
    vox, tm, mod = lax.axis_index("vox"), lax.axis_index("tm"), lax.axis_index("mod")
    z, c4 = vox // PLANE, vox % PLANE
    nplane = PLANE * ntm * nmod
    place = (c4 * ntm + tm) * nmod + mod
    ngram = PLANE * ntm
    gplace = c4 * ntm + tm
    nrhs = PLANE * nmod
    rplace = c4 * nmod + mod
    grow = rank // ngram
    rrow = trs // nrhs
    srow = -(-subjects // nplane)
    own = pl.ds(pl.multiple_of(trs * tm, trs), trs)
    part = rows // ntm
    my_part = pl.ds(pl.multiple_of(part * tm, part), part)

    def far(i):
        return nz // 2 + (1 - 2 * lax.rem(i, 2)) * (i // 2)

    def along_tm(d):
        return (vox, lax.rem(tm + d, ntm), mod)

    def along_z(i):
        d = far(i)
        return (lax.rem(z + d, nz) * PLANE + c4, tm, mod)

    def in_plane(d):
        to = lax.rem(place + d, nplane)
        return (z * PLANE + to // (ntm * nmod), lax.rem(to // nmod, ntm), lax.rem(to, nmod))

    def send(stage, src, dst, device):
        pltpu.make_async_remote_copy(
            src_ref=src,
            dst_ref=dst,
            send_sem=send_sem.at[stage],
            recv_sem=recv_sem.at[stage],
            device_id=device,
            device_id_type=MESH,
        ).start()

    def every(count, body):
        def step(d, carry):
            body(d)
            return carry

        lax.fori_loop(1, count, step, 0)

    def wait(sem, stage, ref):
        pltpu.make_async_copy(ref, ref, sem.at[stage]).wait()

    barrier = pltpu.get_barrier_semaphore()
    every(
        nplane,
        lambda d: pl.semaphore_signal(barrier, 1, device_id=in_plane(d), device_id_type=MESH),
    )
    every(
        nz, lambda d: pl.semaphore_signal(barrier, 1, device_id=along_z(d), device_id_type=MESH)
    )
    own_pad = pl.ds(pl.multiple_of(reach + trs * tm, 8), trs)
    loads = [
        pltpu.make_async_copy(src, dst, local_sem.at[i])
        for i, (src, dst) in enumerate(
            (
                (scans, x_in),
                (subject_in, subject),
                (kept_in, kept),
                (spatial_in, spatial),
                (time_init, pad.at[own_pad]),
            )
        )
    ]
    for load in loads:
        load.start()
    pl.semaphore_wait(barrier, nplane + nz - 2)

    pad[0:reach] = jnp.zeros((reach, rank), jnp.float32)
    every(ntm, lambda d: send(0, time_init, pad.at[own_pad], along_tm(d)))

    for load in loads:
        load.wait()

    def widen(i, carry):
        at = pl.ds(pl.multiple_of(i * 512, 512), 512)
        x_f32[at] = x_in[at].astype(jnp.float32)
        return carry

    lax.fori_loop(0, rows * subjects // 512, widen, 0)

    def regroup(s, carry):
        xs[pl.ds(pl.multiple_of(s * rows, rows), rows)] = x_f32[
            pl.ds(s, rows, subjects), :
        ].astype(jnp.bfloat16)
        return carry

    lax.fori_loop(0, subjects, regroup, 0)
    block = trs // kept.shape[0]
    spot = [lax.broadcasted_iota(jnp.int32, (kept.shape[0], trs), d) for d in range(2)]
    spans = jnp.where(spot[1] // block == spot[0], 1.0, 0.0)
    mask[...] = jnp.where(mod == 0, tdot(kept[...].astype(jnp.float32), spans), 1.0)
    subj = subject[...]
    subj_gram = tdot(subj, subj)
    previous = spatial[...].astype(jnp.bfloat16)
    is_fmri = mod == 0
    lags = [hrf[k] for k in range(reach)]
    taps = [jnp.where(is_fmri, lags[k], 1.0 if k == 0 else 0.0) for k in range(reach)]

    wait(recv_sem, 0, pad.at[pl.ds(reach, (ntm - 1) * trs)])

    def conv(weights, base):
        summed = weights[0] * pad[reach + base : reach + base + trs]
        for k in range(1, reach):
            summed = summed + weights[k] * pad[reach + base - k : reach + base - k + trs]
        return summed

    for i in range(ntm):
        factors[i * trs : (i + 1) * trs] = conv(taps, i * trs)
    factor = factors[own]
    everything = factors[...]
    time_gram = tdot(everything, everything)

    rhs[...] = jnp.zeros_like(rhs)

    def fill_pair(s):
        first = pl.ds(pl.multiple_of(s * rows, rows), rows)
        second = pl.ds(pl.multiple_of((s + 1) * rows, rows), rows)
        khatri = jnp.concatenate(
            [
                (subject[pl.ds(s, 1)] * factor).astype(jnp.bfloat16),
                (subject[pl.ds(s + 1, 1)] * factor).astype(jnp.bfloat16),
            ]
        )
        modeled = lax.dot_general(
            previous, khatri, (((1,), (1,)), ((), ())), preferred_element_type=jnp.float32
        )
        f0 = jnp.where(
            mask[pl.ds(s, 1)] > 0, xs[first].astype(jnp.float32), modeled[:, :trs]
        ).astype(jnp.bfloat16)
        f1 = jnp.where(
            mask[pl.ds(s + 1, 1)] > 0, xs[second].astype(jnp.float32), modeled[:, trs:]
        ).astype(jnp.bfloat16)
        xs[first] = f0
        xs[second] = f1
        rhs[...] += jnp.dot(
            jnp.concatenate([f0, f1], axis=1), khatri, preferred_element_type=jnp.float32
        )

    steps = rank // 8
    turns = math.gcd(subjects // 2, steps)

    def fill(i, mat):
        for j in range(subjects // 2 // turns):
            fill_pair(2 * (i * (subjects // 2 // turns) + j))
        for j in range(steps // turns):
            mat = eliminate(mat)
        return mat

    inverse = lax.fori_loop(0, turns, fill, ridged(subj_gram * time_gram))

    def scatter_rows(d):
        to = pl.multiple_of(part * lax.rem(tm + d, ntm), part)
        send(1, rhs.at[pl.ds(to, part)], rhs_in.at[d - 1], along_tm(d))

    every(ntm, scatter_rows)
    wait(recv_sem, 1, rhs_in)
    mine = rhs[my_part]
    for d in range(ntm - 1):
        mine = mine + rhs_in[d]
    solved = dot(mine, inverse)
    updated[my_part] = solved
    every(ntm, lambda d: send(2, updated.at[my_part], updated.at[my_part], along_tm(d)))

    gram_part[...] = tdot(solved, solved)

    def scatter_gram(d):
        to = lax.rem(gplace + d, ngram)
        send(
            3,
            gram_part.at[pl.ds(pl.multiple_of(grow * to, grow), grow)],
            g1.at[d - 1],
            (z * PLANE + to // ntm, lax.rem(to, ntm), mod),
        )

    every(ngram, scatter_gram)
    wait(recv_sem, 2, updated.at[pl.ds(0, (ntm - 1) * part)])
    upd = updated[...]
    out_spatial[...] = upd

    wait(recv_sem, 3, g1)
    mine = gram_part[pl.ds(pl.multiple_of(grow * gplace, grow), grow)]
    for d in range(ngram - 1):
        mine = mine + g1[d]
    g2[z] = mine
    every(nz, lambda d: send(4, g2.at[z], g2.at[z], along_z(d)))

    def project(i, proj):
        s = 2 * i
        khatri = jnp.concatenate(
            [
                (upd * subject[pl.ds(s, 1)]).astype(jnp.bfloat16),
                (upd * subject[pl.ds(s + 1, 1)]).astype(jnp.bfloat16),
            ]
        )
        filled = xs[pl.ds(pl.multiple_of(s * rows, rows), 2 * rows)]
        return proj + lax.dot_general(
            filled, khatri, (((0,), (0,)), ((), ())), preferred_element_type=jnp.float32
        )

    proj = lax.fori_loop(
        0, subjects // 2, project, jnp.zeros((trs, rank), jnp.float32), unroll=8
    )
    ppad[0:reach] = jnp.zeros((reach, rank), jnp.float32)
    ppad[reach : reach + trs] = proj
    ppad[reach + trs :] = jnp.zeros((reach, rank), jnp.float32)
    spread = taps[0] * ppad[0 : reach + trs]
    for k in range(1, reach):
        spread = spread + taps[k] * ppad[k : k + reach + trs]
    ext[...] = spread

    def scatter_time(d):
        to = lax.rem(rplace + d, nrhs)
        send(
            6,
            ext.at[pl.ds(pl.multiple_of(reach + rrow * to, 8), rrow)],
            r1.at[d - 1],
            (z * PLANE + to // nmod, tm, lax.rem(to, nmod)),
        )

    every(nrhs, scatter_time)
    gives_halo = jnp.logical_and(is_fmri, tm > 0)
    takes_halo = jnp.logical_and(rplace == nrhs - 1, tm < ntm - 1)
    halo_copy = pltpu.make_async_remote_copy(
        src_ref=ext.at[pl.ds(0, rrow)],
        dst_ref=halo.at[c4],
        send_sem=halo_sem.at[0],
        recv_sem=halo_sem.at[1],
        device_id=(z * PLANE + PLANE - 1, lax.rem(tm + ntm - 1, ntm), nmod - 1),
        device_id_type=MESH,
    )
    halo_all = pltpu.make_async_copy(halo, halo, halo_sem.at[1])

    @pl.when(gives_halo)
    def _():
        halo_copy.start()

    wait(recv_sem, 4, g2.at[pl.ds(0, nz - 1)])
    mine = g2[0]
    for i in range(1, nz):
        mine = mine + g2[i]
    g_sum[...] = mine
    g_own = mod * ngram + gplace
    g_all[g_own] = mine
    every(nplane, lambda d: send(5, g_sum, g_all.at[g_own], in_plane(d)))

    wait(recv_sem, 6, r1)
    mine = ext[pl.ds(pl.multiple_of(reach + rrow * rplace, 8), rrow)]
    for d in range(nrhs - 1):
        mine = mine + r1[d]
    r2[z] = mine

    @pl.when(takes_halo)
    def _():
        halo_all.wait()
        total = r2[z]
        for i in range(PLANE):
            total = total + halo[i]
        r2[z] = total

    every(nz, lambda d: send(7, r2.at[z], r2.at[z], along_z(d)))

    wait(recv_sem, 5, g_all.at[pl.ds(0, nplane - 1)])
    grams = [
        jnp.concatenate([g_all[m * ngram + i] for i in range(ngram)]) for m in range(nmod)
    ]
    inverse = eliminations(steps // 2, ridged((grams[0] + grams[1]) * subj_gram))

    wait(recv_sem, 7, r2.at[pl.ds(0, nz - 1)])
    mine = r2[0]
    for i in range(1, nz):
        mine = mine + r2[i]
    r_sum[...] = mine
    r_own = tm * nrhs + rplace
    r_all[r_own] = mine
    every(nplane, lambda d: send(8, r_sum, r_all.at[r_own], in_plane(d)))
    inverse = eliminations(steps - steps // 2, inverse)
    wait(recv_sem, 8, r_all.at[pl.ds(0, nplane - 1)])
    right = jnp.concatenate([r_all[i] for i in range(ntm * nrhs)])
    raw = (rows * nz * PLANE) * dot(right, inverse)
    mean = jnp.sum(raw * raw, axis=0, keepdims=True) / (ntm * trs)
    fresh = raw / jnp.sqrt(mean + EPS)
    scale_c = (2.0 * rows * nz * PLANE * trs * ntm) ** (-0.5)
    pad[reach:] = fresh * scale_c
    win[...] = pad[pl.ds(pl.multiple_of(trs * tm, trs), reach + trs)]
    scaled = taps[0] * win[reach:]
    for k in range(1, reach):
        scaled = scaled + taps[k] * win[reach - k : reach - k + trs]
    high = scaled.astype(jnp.bfloat16)
    low = (scaled - high.astype(jnp.float32)).astype(jnp.bfloat16)
    halves = jnp.concatenate([high, low], axis=1)

    def contract(i, carry):
        lines = []
        for j in range(srow):
            s = i * srow + j
            both = jnp.dot(
                xs[pl.ds(pl.multiple_of(s * rows, rows), rows)],
                halves,
                preferred_element_type=jnp.float32,
            )
            lines.append(
                jnp.sum((both[:, :rank] + both[:, rank:]) * upd, axis=0, keepdims=True)
            )
        s_part[i] = jnp.concatenate(lines)
        return carry

    lax.fori_loop(0, subjects // srow, contract, 0, unroll=6)
    for i in range(subjects // srow, nplane):
        s_part[i] = jnp.zeros((srow, rank), jnp.float32)
    every(
        nplane,
        lambda d: send(9, s_part.at[lax.rem(place + d, nplane)], s1.at[d - 1], in_plane(d)),
    )
    for i in range(ntm):
        factors[i * trs : (i + 1) * trs] = conv(lags, i * trs)
    eeg = pad[reach:]
    fmri = factors[...]
    pad[reach:] = fresh
    out_time[...] = pad[own_pad]
    gram_c = grams[0] * tdot(fmri, fmri) + grams[1] * tdot(eeg, eeg)

    wait(recv_sem, 9, s1)
    mine = s_part[place]
    for d in range(nplane - 1):
        mine = mine + s1[d]
    s2[z] = mine
    every(nz, lambda d: send(10, s2.at[z], s2.at[z], along_z(d)))
    inverse = eliminations(steps, ridged(gram_c))
    wait(recv_sem, 10, s2.at[pl.ds(0, nz - 1)])
    mine = s2[0]
    for i in range(1, nz):
        mine = mine + s2[i]
    s_sum[...] = mine
    s_all[place] = mine
    every(nplane, lambda d: send(11, s_sum, s_all.at[place], in_plane(d)))
    wait(recv_sem, 11, s_all.at[pl.ds(0, nplane - 1)])
    out_subject[...] = dot(
        jnp.concatenate([s_all[i] for i in range(subjects // srow)]), inverse
    )

    wait(send_sem, 0, pad.at[pl.ds(reach, (ntm - 1) * trs)])
    wait(send_sem, 1, rhs_in)
    wait(send_sem, 2, updated.at[pl.ds(0, (ntm - 1) * part)])
    wait(send_sem, 3, g1)
    wait(send_sem, 4, g2.at[pl.ds(0, nz - 1)])
    wait(send_sem, 5, g_all.at[pl.ds(0, nplane - 1)])
    wait(send_sem, 6, r1)
    wait(send_sem, 7, r2.at[pl.ds(0, nz - 1)])
    wait(send_sem, 8, r_all.at[pl.ds(0, nplane - 1)])
    wait(send_sem, 9, s1)
    wait(send_sem, 10, s2.at[pl.ds(0, nz - 1)])
    wait(send_sem, 11, s_all.at[pl.ds(0, nplane - 1)])

    @pl.when(gives_halo)
    def _():
        halo_copy.wait_send()


def per_device(scans, spatial_init, time_init, subject_init, hrf_kernel, kept_blocks):
    nz = lax.axis_size("vox") // PLANE
    ntm, nmod = lax.axis_size("tm"), lax.axis_size("mod")
    _, rows, subjects, trs = scans.shape
    rank = subject_init.shape[1]
    reach = hrf_kernel.shape[0]
    nplane, ngram, nrhs = PLANE * ntm * nmod, PLANE * ntm, PLANE * nmod
    grow, rrow, srow = rank // ngram, trs // nrhs, -(-subjects // nplane)
    f32, bf16 = jnp.float32, jnp.bfloat16
    anywhere = pl.BlockSpec(memory_space=pl.ANY)
    updated, time_factors, subject_factors = pl.pallas_call(
        functools.partial(sweep, (nz, ntm, nmod)),
        out_shape=(
            jax.ShapeDtypeStruct((rows, rank), f32),
            jax.ShapeDtypeStruct((trs, rank), f32),
            jax.ShapeDtypeStruct((subjects, rank), f32),
        ),
        in_specs=[anywhere] * 4 + [pl.BlockSpec(memory_space=pltpu.SMEM), anywhere],
        out_specs=(pl.BlockSpec(memory_space=pltpu.VMEM),) * 3,
        scratch_shapes=[
            pltpu.VMEM((rows, rank), f32),
            pltpu.VMEM((subjects, rank), f32),
            pltpu.VMEM(kept_blocks.shape[::-1], jnp.int32),
            pltpu.VMEM((reach + trs, rank), f32),
            pltpu.VMEM((rows * subjects, trs), bf16),
            pltpu.VMEM((rows * subjects, trs), f32),
            pltpu.VMEM((subjects * rows, trs), bf16),
            pltpu.VMEM((subjects, trs), f32),
            pltpu.VMEM((reach + ntm * trs, rank), f32),
            pltpu.VMEM((ntm * trs, rank), f32),
            pltpu.VMEM((rows, rank), f32),
            pltpu.VMEM((ntm - 1, rows // ntm, rank), f32),
            pltpu.VMEM((rows, rank), f32),
            pltpu.VMEM((rank, rank), f32),
            pltpu.VMEM((ngram - 1, grow, rank), f32),
            pltpu.VMEM((nz, grow, rank), f32),
            pltpu.VMEM((grow, rank), f32),
            pltpu.VMEM((nplane, grow, rank), f32),
            pltpu.VMEM((2 * reach + trs, rank), f32),
            pltpu.VMEM((reach + trs, rank), f32),
            pltpu.VMEM((PLANE, rrow, rank), f32),
            pltpu.VMEM((nrhs - 1, rrow, rank), f32),
            pltpu.VMEM((nz, rrow, rank), f32),
            pltpu.VMEM((rrow, rank), f32),
            pltpu.VMEM((nplane, rrow, rank), f32),
            pltpu.VMEM((nplane, srow, rank), f32),
            pltpu.VMEM((nplane - 1, srow, rank), f32),
            pltpu.VMEM((nz, srow, rank), f32),
            pltpu.VMEM((srow, rank), f32),
            pltpu.VMEM((nplane, srow, rank), f32),
            pltpu.SemaphoreType.DMA((5,)),
            pltpu.SemaphoreType.DMA((12,)),
            pltpu.SemaphoreType.DMA((12,)),
            pltpu.SemaphoreType.DMA((2,)),
        ],
        compiler_params=pltpu.CompilerParams(
            collective_id=0, has_side_effects=True, vmem_limit_bytes=62 * 1024 * 1024
        ),
        name="sweep",
    )(
        scans.reshape(rows * subjects, trs),
        spatial_init[0],
        time_init,
        subject_init,
        hrf_kernel,
        kept_blocks.T,
    )
    return updated[None], time_factors, subject_factors


def solution(mesh):
    return jax.shard_map(
        per_device,
        mesh=mesh,
        in_specs=(
            P("mod", "vox", None, "tm"),
            P("mod", "vox", None),
            P("tm", None),
            P(),
            P(),
            P(None, "tm"),
        ),
        out_specs=(P("mod", "vox", None), P("tm", None), P()),
        check_vma=False,
    )
```

```python
import functools
import math

import jax
import jax.numpy as jnp
from jax import lax
from jax.experimental import pallas as pl
from jax.experimental.pallas import tpu as pltpu
from jax.sharding import PartitionSpec as P

RIDGE = 0.1
EPS = 1e-06
MESH = pl.DeviceIdType.MESH
PLANE = 4
HIGHEST = lax.Precision.HIGHEST


def dot(a, b):
    return jnp.dot(a, b, precision=HIGHEST, preferred_element_type=jnp.float32)


def tdot(a, b):
    return lax.dot_general(
        a, b, (((0,), (0,)), ((), ())), precision=HIGHEST, preferred_element_type=jnp.float32
    )


def ridged(gram):
    n = gram.shape[0]
    at = [lax.broadcasted_iota(jnp.int32, (n, n), d) for d in range(2)]
    return gram + jnp.where(at[0] == at[1], RIDGE, 0.0)


def eliminate(mat):
    n = mat.shape[0]
    lane = lax.broadcasted_iota(jnp.int32, (8, n), 1)
    sub = lax.broadcasted_iota(jnp.int32, (8, n), 0)
    inside = lane < 8
    top = mat[0:8]
    cols = [jnp.broadcast_to(top[:, j : j + 1], (8, n)) for j in range(8)]
    row = jnp.where(inside, jnp.where(lane == sub, 1.0, 0.0), top)
    for i in range(8):
        gain = jnp.where(sub == i, -1.0, cols[i]) * (1.0 / cols[i][i : i + 1])
        row = jnp.where(sub == i, 0.0, row) - gain * row[i : i + 1]
        for j in range(i + 1, 8):
            cols[j] = jnp.where(sub == i, 0.0, cols[j]) - gain * cols[j][i : i + 1]
    rows = []
    for b in range(1, n // 8):
        below = mat[8 * b : 8 * b + 8]
        left = jnp.where(inside, 0.0, below)
        for j in range(8):
            left = left - jnp.broadcast_to(below[:, j : j + 1], (8, n)) * row[j : j + 1]
        rows.append(left)
    return pltpu.roll(jnp.concatenate(rows + [row]), n - 8, 1)


def eliminations(count, mat):
    return lax.fori_loop(0, count, lambda _, m: eliminate(m), mat, unroll=2)


def sweep(
    sizes,
    scans,
    spatial_in,
    time_init,
    subject_in,
    hrf,
    kept_in,
    out_spatial,
    out_time,
    out_subject,
    spatial,
    subject,
    kept,
    win,
    x_in,
    x_f32,
    xs,
    mask,
    pad,
    factors,
    rhs,
    rhs_in,
    updated,
    gram_part,
    g1,
    g2,
    g_sum,
    g_all,
    ppad,
    ext,
    halo,
    r1,
    r2,
    r_sum,
    r_all,
    s_part,
    s1,
    s2,
    s_sum,
    s_all,
    local_sem,
    send_sem,
    recv_sem,
    halo_sem,
):
    nz, ntm, nmod = sizes
    rows, rank = spatial.shape
    subjects = subject.shape[0]
    trs = time_init.shape[0]
    reach = hrf.shape[0]
    vox, tm, mod = lax.axis_index("vox"), lax.axis_index("tm"), lax.axis_index("mod")
    z, c4 = vox // PLANE, vox % PLANE
    nplane = PLANE * ntm * nmod
    place = (c4 * ntm + tm) * nmod + mod
    ngram = PLANE * ntm
    gplace = c4 * ntm + tm
    nrhs = PLANE * nmod
    rplace = c4 * nmod + mod
    grow = rank // ngram
    rrow = trs // nrhs
    srow = -(-subjects // nplane)
    own = pl.ds(pl.multiple_of(trs * tm, trs), trs)
    part = rows // ntm
    my_part = pl.ds(pl.multiple_of(part * tm, part), part)

    def far(i):
        return nz // 2 + (1 - 2 * lax.rem(i, 2)) * (i // 2)

    def along_tm(d):
        return (vox, lax.rem(tm + d, ntm), mod)

    def along_z(i):
        d = far(i)
        return (lax.rem(z + d, nz) * PLANE + c4, tm, mod)

    def in_plane(d):
        to = lax.rem(place + d, nplane)
        return (z * PLANE + to // (ntm * nmod), lax.rem(to // nmod, ntm), lax.rem(to, nmod))

    def send(stage, src, dst, device):
        pltpu.make_async_remote_copy(
            src_ref=src,
            dst_ref=dst,
            send_sem=send_sem.at[stage],
            recv_sem=recv_sem.at[stage],
            device_id=device,
            device_id_type=MESH,
        ).start()

    def every(count, body):
        def step(d, carry):
            body(d)
            return carry

        lax.fori_loop(1, count, step, 0)

    def wait(sem, stage, ref):
        pltpu.make_async_copy(ref, ref, sem.at[stage]).wait()

    barrier = pltpu.get_barrier_semaphore()
    every(
        nplane,
        lambda d: pl.semaphore_signal(barrier, 1, device_id=in_plane(d), device_id_type=MESH),
    )
    every(
        nz, lambda d: pl.semaphore_signal(barrier, 1, device_id=along_z(d), device_id_type=MESH)
    )
    own_pad = pl.ds(pl.multiple_of(reach + trs * tm, 8), trs)
    loads = [
        pltpu.make_async_copy(src, dst, local_sem.at[i])
        for i, (src, dst) in enumerate(
            (
                (scans, x_in),
                (subject_in, subject),
                (kept_in, kept),
                (spatial_in, spatial),
                (time_init, pad.at[own_pad]),
            )
        )
    ]
    for load in loads:
        load.start()
    pl.semaphore_wait(barrier, nplane + nz - 2)

    pad[0:reach] = jnp.zeros((reach, rank), jnp.float32)
    every(ntm, lambda d: send(0, time_init, pad.at[own_pad], along_tm(d)))

    for load in loads:
        load.wait()

    def widen(i, carry):
        at = pl.ds(pl.multiple_of(i * 512, 512), 512)
        x_f32[at] = x_in[at].astype(jnp.float32)
        return carry

    lax.fori_loop(0, rows * subjects // 512, widen, 0)

    def regroup(s, carry):
        xs[pl.ds(pl.multiple_of(s * rows, rows), rows)] = x_f32[
            pl.ds(s, rows, subjects), :
        ].astype(jnp.bfloat16)
        return carry

    lax.fori_loop(0, subjects, regroup, 0)
    block = trs // kept.shape[0]
    spot = [lax.broadcasted_iota(jnp.int32, (kept.shape[0], trs), d) for d in range(2)]
    spans = jnp.where(spot[1] // block == spot[0], 1.0, 0.0)
    mask[...] = jnp.where(mod == 0, tdot(kept[...].astype(jnp.float32), spans), 1.0)
    subj = subject[...]
    subj_gram = tdot(subj, subj)
    previous = spatial[...].astype(jnp.bfloat16)
    is_fmri = mod == 0
    lags = [hrf[k] for k in range(reach)]
    taps = [jnp.where(is_fmri, lags[k], 1.0 if k == 0 else 0.0) for k in range(reach)]

    wait(recv_sem, 0, pad.at[pl.ds(reach, (ntm - 1) * trs)])

    def conv(weights, base):
        summed = weights[0] * pad[reach + base : reach + base + trs]
        for k in range(1, reach):
            summed = summed + weights[k] * pad[reach + base - k : reach + base - k + trs]
        return summed

    for i in range(ntm):
        factors[i * trs : (i + 1) * trs] = conv(taps, i * trs)
    factor = factors[own]
    everything = factors[...]
    time_gram = tdot(everything, everything)

    rhs[...] = jnp.zeros_like(rhs)

    def fill_pair(s):
        first = pl.ds(pl.multiple_of(s * rows, rows), rows)
        second = pl.ds(pl.multiple_of((s + 1) * rows, rows), rows)
        khatri = jnp.concatenate(
            [
                (subject[pl.ds(s, 1)] * factor).astype(jnp.bfloat16),
                (subject[pl.ds(s + 1, 1)] * factor).astype(jnp.bfloat16),
            ]
        )
        modeled = lax.dot_general(
            previous, khatri, (((1,), (1,)), ((), ())), preferred_element_type=jnp.float32
        )
        f0 = jnp.where(
            mask[pl.ds(s, 1)] > 0, xs[first].astype(jnp.float32), modeled[:, :trs]
        ).astype(jnp.bfloat16)
        f1 = jnp.where(
            mask[pl.ds(s + 1, 1)] > 0, xs[second].astype(jnp.float32), modeled[:, trs:]
        ).astype(jnp.bfloat16)
        xs[first] = f0
        xs[second] = f1
        rhs[...] += jnp.dot(
            jnp.concatenate([f0, f1], axis=1), khatri, preferred_element_type=jnp.float32
        )

    steps = rank // 8
    turns = math.gcd(subjects // 2, steps // 2)

    def fill(i, mat):
        for j in range(subjects // 2 // turns):
            fill_pair(2 * (i * (subjects // 2 // turns) + j))
        for j in range(steps // 2 // turns):
            mat = eliminate(mat)
        return mat

    inverse = lax.fori_loop(0, turns, fill, ridged(subj_gram * time_gram))

    def scatter_rows(d):
        to = pl.multiple_of(part * lax.rem(tm + d, ntm), part)
        send(1, rhs.at[pl.ds(to, part)], rhs_in.at[d - 1], along_tm(d))

    every(ntm, scatter_rows)
    inverse = eliminations(steps - steps // 2, inverse)
    wait(recv_sem, 1, rhs_in)
    mine = rhs[my_part]
    for d in range(ntm - 1):
        mine = mine + rhs_in[d]
    solved = dot(mine, inverse)
    updated[my_part] = solved
    every(ntm, lambda d: send(2, updated.at[my_part], updated.at[my_part], along_tm(d)))

    gram_part[...] = tdot(solved, solved)

    def scatter_gram(d):
        to = lax.rem(gplace + d, ngram)
        send(
            3,
            gram_part.at[pl.ds(pl.multiple_of(grow * to, grow), grow)],
            g1.at[d - 1],
            (z * PLANE + to // ntm, lax.rem(to, ntm), mod),
        )

    every(ngram, scatter_gram)
    wait(recv_sem, 2, updated.at[pl.ds(0, (ntm - 1) * part)])
    upd = updated[...]
    out_spatial[...] = upd

    wait(recv_sem, 3, g1)
    mine = gram_part[pl.ds(pl.multiple_of(grow * gplace, grow), grow)]
    for d in range(ngram - 1):
        mine = mine + g1[d]
    g2[z] = mine
    every(nz, lambda d: send(4, g2.at[z], g2.at[z], along_z(d)))

    def project(i, proj):
        s = 2 * i
        khatri = jnp.concatenate(
            [
                (upd * subject[pl.ds(s, 1)]).astype(jnp.bfloat16),
                (upd * subject[pl.ds(s + 1, 1)]).astype(jnp.bfloat16),
            ]
        )
        filled = xs[pl.ds(pl.multiple_of(s * rows, rows), 2 * rows)]
        return proj + lax.dot_general(
            filled, khatri, (((0,), (0,)), ((), ())), preferred_element_type=jnp.float32
        )

    proj = lax.fori_loop(
        0, subjects // 2, project, jnp.zeros((trs, rank), jnp.float32), unroll=8
    )
    ppad[0:reach] = jnp.zeros((reach, rank), jnp.float32)
    ppad[reach : reach + trs] = proj
    ppad[reach + trs :] = jnp.zeros((reach, rank), jnp.float32)
    spread = taps[0] * ppad[0 : reach + trs]
    for k in range(1, reach):
        spread = spread + taps[k] * ppad[k : k + reach + trs]
    ext[...] = spread

    def scatter_time(d):
        to = lax.rem(rplace + d, nrhs)
        send(
            6,
            ext.at[pl.ds(pl.multiple_of(reach + rrow * to, 8), rrow)],
            r1.at[d - 1],
            (z * PLANE + to // nmod, tm, lax.rem(to, nmod)),
        )

    every(nrhs, scatter_time)
    gives_halo = jnp.logical_and(is_fmri, tm > 0)
    takes_halo = jnp.logical_and(rplace == nrhs - 1, tm < ntm - 1)
    halo_copy = pltpu.make_async_remote_copy(
        src_ref=ext.at[pl.ds(0, rrow)],
        dst_ref=halo.at[c4],
        send_sem=halo_sem.at[0],
        recv_sem=halo_sem.at[1],
        device_id=(z * PLANE + PLANE - 1, lax.rem(tm + ntm - 1, ntm), nmod - 1),
        device_id_type=MESH,
    )
    halo_all = pltpu.make_async_copy(halo, halo, halo_sem.at[1])

    @pl.when(gives_halo)
    def _():
        halo_copy.start()

    wait(recv_sem, 4, g2.at[pl.ds(0, nz - 1)])
    mine = g2[0]
    for i in range(1, nz):
        mine = mine + g2[i]
    g_sum[...] = mine
    g_own = mod * ngram + gplace
    g_all[g_own] = mine
    every(nplane, lambda d: send(5, g_sum, g_all.at[g_own], in_plane(d)))

    wait(recv_sem, 6, r1)
    mine = ext[pl.ds(pl.multiple_of(reach + rrow * rplace, 8), rrow)]
    for d in range(nrhs - 1):
        mine = mine + r1[d]
    r2[z] = mine

    @pl.when(takes_halo)
    def _():
        halo_all.wait()
        total = r2[z]
        for i in range(PLANE):
            total = total + halo[i]
        r2[z] = total

    every(nz, lambda d: send(7, r2.at[z], r2.at[z], along_z(d)))

    wait(recv_sem, 5, g_all.at[pl.ds(0, nplane - 1)])
    grams = [
        jnp.concatenate([g_all[m * ngram + i] for i in range(ngram)]) for m in range(nmod)
    ]
    inverse = eliminations(steps // 8, ridged((grams[0] + grams[1]) * subj_gram))

    wait(recv_sem, 7, r2.at[pl.ds(0, nz - 1)])
    mine = r2[0]
    for i in range(1, nz):
        mine = mine + r2[i]
    r_sum[...] = mine
    r_own = tm * nrhs + rplace
    r_all[r_own] = mine
    every(nplane, lambda d: send(8, r_sum, r_all.at[r_own], in_plane(d)))
    inverse = eliminations(steps - steps // 8, inverse)
    wait(recv_sem, 8, r_all.at[pl.ds(0, nplane - 1)])
    right = jnp.concatenate([r_all[i] for i in range(ntm * nrhs)])
    raw = (rows * nz * PLANE) * dot(right, inverse)
    mean = jnp.sum(raw * raw, axis=0, keepdims=True) / (ntm * trs)
    fresh = raw / jnp.sqrt(mean + EPS)
    scale_c = (2.0 * rows * nz * PLANE * trs * ntm) ** (-0.5)
    pad[reach:] = fresh * scale_c
    win[...] = pad[pl.ds(pl.multiple_of(trs * tm, trs), reach + trs)]
    scaled = taps[0] * win[reach:]
    for k in range(1, reach):
        scaled = scaled + taps[k] * win[reach - k : reach - k + trs]
    high = scaled.astype(jnp.bfloat16)
    low = (scaled - high.astype(jnp.float32)).astype(jnp.bfloat16)
    halves = jnp.concatenate([high, low], axis=1)

    def contract(i, carry):
        lines = []
        for j in range(srow):
            s = i * srow + j
            both = jnp.dot(
                xs[pl.ds(pl.multiple_of(s * rows, rows), rows)],
                halves,
                preferred_element_type=jnp.float32,
            )
            lines.append(
                jnp.sum((both[:, :rank] + both[:, rank:]) * upd, axis=0, keepdims=True)
            )
        s_part[i] = jnp.concatenate(lines)
        return carry

    lax.fori_loop(0, subjects // srow, contract, 0, unroll=6)
    for i in range(subjects // srow, nplane):
        s_part[i] = jnp.zeros((srow, rank), jnp.float32)
    every(
        nplane,
        lambda d: send(9, s_part.at[lax.rem(place + d, nplane)], s1.at[d - 1], in_plane(d)),
    )
    for i in range(ntm):
        factors[i * trs : (i + 1) * trs] = conv(lags, i * trs)
    eeg = pad[reach:]
    fmri = factors[...]
    pad[reach:] = fresh
    out_time[...] = pad[own_pad]
    gram_c = grams[0] * tdot(fmri, fmri) + grams[1] * tdot(eeg, eeg)

    wait(recv_sem, 9, s1)
    mine = s_part[place]
    for d in range(nplane - 1):
        mine = mine + s1[d]
    s2[z] = mine
    every(nz, lambda d: send(10, s2.at[z], s2.at[z], along_z(d)))
    inverse = eliminations(steps, ridged(gram_c))
    wait(recv_sem, 10, s2.at[pl.ds(0, nz - 1)])
    mine = s2[0]
    for i in range(1, nz):
        mine = mine + s2[i]
    s_sum[...] = mine
    s_all[place] = mine
    every(nplane, lambda d: send(11, s_sum, s_all.at[place], in_plane(d)))
    wait(recv_sem, 11, s_all.at[pl.ds(0, nplane - 1)])
    out_subject[...] = dot(
        jnp.concatenate([s_all[i] for i in range(subjects // srow)]), inverse
    )

    wait(send_sem, 0, pad.at[pl.ds(reach, (ntm - 1) * trs)])
    wait(send_sem, 1, rhs_in)
    wait(send_sem, 2, updated.at[pl.ds(0, (ntm - 1) * part)])
    wait(send_sem, 3, g1)
    wait(send_sem, 4, g2.at[pl.ds(0, nz - 1)])
    wait(send_sem, 5, g_all.at[pl.ds(0, nplane - 1)])
    wait(send_sem, 6, r1)
    wait(send_sem, 7, r2.at[pl.ds(0, nz - 1)])
    wait(send_sem, 8, r_all.at[pl.ds(0, nplane - 1)])
    wait(send_sem, 9, s1)
    wait(send_sem, 10, s2.at[pl.ds(0, nz - 1)])
    wait(send_sem, 11, s_all.at[pl.ds(0, nplane - 1)])

    @pl.when(gives_halo)
    def _():
        halo_copy.wait_send()


def per_device(scans, spatial_init, time_init, subject_init, hrf_kernel, kept_blocks):
    nz = lax.axis_size("vox") // PLANE
    ntm, nmod = lax.axis_size("tm"), lax.axis_size("mod")
    _, rows, subjects, trs = scans.shape
    rank = subject_init.shape[1]
    reach = hrf_kernel.shape[0]
    nplane, ngram, nrhs = PLANE * ntm * nmod, PLANE * ntm, PLANE * nmod
    grow, rrow, srow = rank // ngram, trs // nrhs, -(-subjects // nplane)
    f32, bf16 = jnp.float32, jnp.bfloat16
    anywhere = pl.BlockSpec(memory_space=pl.ANY)
    updated, time_factors, subject_factors = pl.pallas_call(
        functools.partial(sweep, (nz, ntm, nmod)),
        out_shape=(
            jax.ShapeDtypeStruct((rows, rank), f32),
            jax.ShapeDtypeStruct((trs, rank), f32),
            jax.ShapeDtypeStruct((subjects, rank), f32),
        ),
        in_specs=[anywhere] * 4 + [pl.BlockSpec(memory_space=pltpu.SMEM), anywhere],
        out_specs=(pl.BlockSpec(memory_space=pltpu.VMEM),) * 3,
        scratch_shapes=[
            pltpu.VMEM((rows, rank), f32),
            pltpu.VMEM((subjects, rank), f32),
            pltpu.VMEM(kept_blocks.shape[::-1], jnp.int32),
            pltpu.VMEM((reach + trs, rank), f32),
            pltpu.VMEM((rows * subjects, trs), bf16),
            pltpu.VMEM((rows * subjects, trs), f32),
            pltpu.VMEM((subjects * rows, trs), bf16),
            pltpu.VMEM((subjects, trs), f32),
            pltpu.VMEM((reach + ntm * trs, rank), f32),
            pltpu.VMEM((ntm * trs, rank), f32),
            pltpu.VMEM((rows, rank), f32),
            pltpu.VMEM((ntm - 1, rows // ntm, rank), f32),
            pltpu.VMEM((rows, rank), f32),
            pltpu.VMEM((rank, rank), f32),
            pltpu.VMEM((ngram - 1, grow, rank), f32),
            pltpu.VMEM((nz, grow, rank), f32),
            pltpu.VMEM((grow, rank), f32),
            pltpu.VMEM((nplane, grow, rank), f32),
            pltpu.VMEM((2 * reach + trs, rank), f32),
            pltpu.VMEM((reach + trs, rank), f32),
            pltpu.VMEM((PLANE, rrow, rank), f32),
            pltpu.VMEM((nrhs - 1, rrow, rank), f32),
            pltpu.VMEM((nz, rrow, rank), f32),
            pltpu.VMEM((rrow, rank), f32),
            pltpu.VMEM((nplane, rrow, rank), f32),
            pltpu.VMEM((nplane, srow, rank), f32),
            pltpu.VMEM((nplane - 1, srow, rank), f32),
            pltpu.VMEM((nz, srow, rank), f32),
            pltpu.VMEM((srow, rank), f32),
            pltpu.VMEM((nplane, srow, rank), f32),
            pltpu.SemaphoreType.DMA((5,)),
            pltpu.SemaphoreType.DMA((12,)),
            pltpu.SemaphoreType.DMA((12,)),
            pltpu.SemaphoreType.DMA((2,)),
        ],
        compiler_params=pltpu.CompilerParams(
            collective_id=0, has_side_effects=True, vmem_limit_bytes=62 * 1024 * 1024
        ),
        name="sweep",
    )(
        scans.reshape(rows * subjects, trs),
        spatial_init[0],
        time_init,
        subject_init,
        hrf_kernel,
        kept_blocks.T,
    )
    return updated[None], time_factors, subject_factors


def solution(mesh):
    return jax.shard_map(
        per_device,
        mesh=mesh,
        in_specs=(
            P("mod", "vox", None, "tm"),
            P("mod", "vox", None),
            P("tm", None),
            P(),
            P(),
            P(None, "tm"),
        ),
        out_specs=(P("mod", "vox", None), P("tm", None), P()),
        check_vma=False,
    )
```
